32 devices in a mesh: depth: 2 (over x), row: 4 (over y, core), col: 4 (over z).
Axes of the slice: x: 2, y: 2, z: 4, core: 2. Of those that a mesh axis runs over, the one named last changes fastest.
Arguments:
- inputs: bfloat16 [1280, 4096], P(('depth', 'col'), 'row'), may hold values from -6 to 6
- in_bits: int32 [1280, 4096], P(('depth', 'col'), 'row'), may hold values from 0 to 1
- out_grads: bfloat16 [1280, 14336], P(('depth', 'row'), 'col'), may hold values from -6 to 6
- out_bits: int32 [1280, 14336], P(('depth', 'row'), 'col'), may hold values from 0 to 1
- mean_weight: bfloat16 [14336, 4096], P(('col', 'depth'), 'row'), may hold values from -0.09375 to 0.09375
- sigma_weight: bfloat16 [14336, 4096], P(('col', 'depth'), 'row'), may hold values from 0.0049743652 to 0.049804688
- noise: bfloat16 [14336, 4096], P(('col', 'depth'), 'row'), may hold values from -6 to 6
Outputs:
- input_grad: bfloat16 [1280, 4096], P(('depth', 'col'), 'row')
- mean_grad: float32 [14336, 4096], P(('col', 'depth'), 'row')
- sigma_grad: float32 [14336, 4096], P(('col', 'depth'), 'row')
The draws below stay inside these ranges and needn't reach their ends.
All inputs are finite; a program needn't handle non-finite values.
Results may differ from the reference program's by a relative error of at most 0.017.
Values may be sent and summed in bfloat16 or wider, within the bound.
No kernel may reach another device: no remote copies, remote signals or barrier semaphores. Data moves between devices by JAX's collectives and lax.ppermute only.
A program may use at most 128 MiB of HBM per device.

```python
import math
import jax
import jax.numpy as jnp
from jax import lax

D = 4096
FF = 14336
SLAB = 640
TOKENS = 1280
N_DEPTH = 2


def set_ends(values, rng, least, largest):
    place = [jax.random.randint(jax.random.fold_in(rng, axis), (), 0, length) for axis, length in enumerate(values.shape)]
    main_axis = values.shape.index(max(values.shape))
    neighbour = place[:main_axis] + [(place[main_axis] + 1) % values.shape[main_axis]] + place[main_axis + 1:]
    return values.at[tuple(place)].set(least).at[tuple(neighbour)].set(largest)


def level_of(key, shape, split, low, high):
    level = 1.0
    for dim, parts in split:
        draws = jax.random.uniform(jax.random.fold_in(jax.random.fold_in(key, 6), dim), (parts,), jnp.float32, low / len(split), high / len(split))
        level = level * jnp.repeat(jnp.exp(draws), shape[dim] // parts).reshape((-1,) + (1,) * (len(shape) - 1 - dim))
    return level


def centred(own_key, shape, spread, limit, cuts=(), kind=jnp.bfloat16):
    level = level_of(own_key, shape, cuts, -0.22, 0.18) if cuts else 1.0
    values = jax.random.normal(own_key, shape, jnp.float32) * spread * level
    return jnp.minimum(jnp.maximum(values, -limit), limit).astype(kind)


def setup_inputs(seed: int = 0) -> dict:
    key_of = jax.random.split(jax.random.key(seed), 8)
    inputs = centred(key_of[0], (TOKENS, D), 1.0, 6.0, ((0, 8), (1, 4)))
    in_bits = set_ends(jax.random.randint(key_of[1], (TOKENS, D), 0, 2), jax.random.fold_in(key_of[1], 1), 0, 1).astype(jnp.int32)
    out_grads = centred(key_of[2], (TOKENS, FF), 1.0, 6.0, ((0, 8), (1, 4)))
    out_bits = set_ends(jax.random.randint(key_of[3], (TOKENS, FF), 0, 2), jax.random.fold_in(key_of[3], 1), 0, 1).astype(jnp.int32)
    mean_weight = centred(key_of[4], (FF, D), D ** -0.5, 0.09375, ((0, 8), (1, 4)))
    sigma_weight = jnp.clip(jnp.exp(math.log(0.049804688) - 2.3038113 * jax.random.uniform(key_of[5], (FF, D), jnp.float32) ** level_of(key_of[5], (FF, D), ((0, 8), (1, 4)), -0.2, 0.2)), 0.0049743652, 0.049804688).astype(jnp.bfloat16)
    noise = centred(key_of[6], (FF, D), 1.0, 6.0, ((0, 8), (1, 4)))
    return dict(inputs=inputs, in_bits=in_bits, out_grads=out_grads, out_bits=out_bits, mean_weight=mean_weight, sigma_weight=sigma_weight, noise=noise)


def reference(inputs, in_bits, out_grads, out_bits, mean_weight, sigma_weight, noise):
    in_sign = (1 - 2 * in_bits).astype(jnp.bfloat16)
    signed_inputs = inputs * in_sign
    signed_grads = out_grads * (1 - 2 * out_bits).astype(jnp.bfloat16)
    perturbed = (sigma_weight.astype(jnp.float32) * noise.astype(jnp.float32)).astype(jnp.bfloat16)
    part_a = jnp.dot(out_grads, mean_weight, preferred_element_type=jnp.float32)
    part_b = jnp.dot(signed_grads, perturbed, preferred_element_type=jnp.float32)
    input_grad = (part_a + part_b * in_sign.astype(jnp.float32)).astype(jnp.bfloat16)

    slab_parts = (inputs.reshape(N_DEPTH, SLAB, D), signed_inputs.reshape(N_DEPTH, SLAB, D),
                  out_grads.reshape(N_DEPTH, SLAB, FF), signed_grads.reshape(N_DEPTH, SLAB, FF))
    dims = (((0,), (0,)), ((), ()))

    def accumulate_slab(running, slab):
        feat_a, feat_b, grad_a, grad_b = slab
        mean_partial = lax.dot_general(grad_a, feat_a, dims, preferred_element_type=jnp.float32).astype(jnp.bfloat16)
        sigma_partial = lax.dot_general(grad_b, feat_b, dims, preferred_element_type=jnp.float32).astype(jnp.bfloat16)
        mean_partial = lax.optimization_barrier(mean_partial)
        sigma_partial = lax.optimization_barrier(sigma_partial)
        return (running[0] + mean_partial.astype(jnp.float32), running[1] + sigma_partial.astype(jnp.float32)), None

    zero_sum = jnp.zeros((FF, D), jnp.float32)
    sums, unused = lax.scan(accumulate_slab, (zero_sum, zero_sum), slab_parts)
    grad_scale = TOKENS ** -0.5
    mean_grad = sums[0] * grad_scale
    sigma_grad = sums[1] * grad_scale * noise.astype(jnp.float32)
    return input_grad, mean_grad, sigma_grad
```

```python
import functools

import jax
import jax.numpy as jnp
from jax import lax
from jax.experimental import pallas as pl
from jax.experimental.pallas import tpu as pltpu
from jax.sharding import PartitionSpec as P

VMEM_LIMIT = 56 * 1024 * 1024


def grad_kernel(n_piece, row_ref, *refs):
    pieces, (mean_ref, pert_ref, sign_ref, out_ref, both, sems) = refs[:n_piece], refs[n_piece:]

    @pl.when(pl.program_id(0) == 0)
    def _():
        copies = [
            pltpu.make_async_copy(pieces[k], both.at[row_ref[0] ^ k], sems.at[k])
            for k in range(n_piece)
        ]
        for copy in copies:
            copy.start()
        for copy in copies:
            copy.wait()

    tokens, hidden = sign_ref.shape[0], mean_ref.shape[0]
    grads = both[:, 0].reshape(tokens, hidden)
    signed = both[:, 1].reshape(tokens, hidden)
    part_a = jnp.dot(grads, mean_ref[...], preferred_element_type=jnp.float32)
    part_b = jnp.dot(signed, pert_ref[...], preferred_element_type=jnp.float32)
    out_ref[...] = (part_a + part_b * sign_ref[...].astype(jnp.float32)).astype(out_ref.dtype)


def partial_input_grad(row, pieces, mean_weight, perturbed, sign):
    hidden, feats = mean_weight.shape
    tokens = sign.shape[0]
    n_piece = len(pieces)
    tile = min(256, feats)
    any_spec = pl.BlockSpec(memory_space=pl.ANY)
    return pl.pallas_call(
        functools.partial(grad_kernel, n_piece),
        grid_spec=pltpu.PrefetchScalarGridSpec(
            num_scalar_prefetch=1,
            grid=(feats // tile,),
            in_specs=[any_spec] * n_piece
            + [
                pl.BlockSpec((hidden, tile), lambda f, row: (0, f)),
                pl.BlockSpec((hidden, tile), lambda f, row: (0, f)),
                pl.BlockSpec((tokens, tile), lambda f, row: (0, f)),
            ],
            out_specs=pl.BlockSpec((tokens, tile), lambda f, row: (0, f)),
            scratch_shapes=[
                pltpu.VMEM((n_piece,) + pieces[0].shape, jnp.bfloat16),
                pltpu.SemaphoreType.DMA((n_piece,)),
            ],
        ),
        out_shape=jax.ShapeDtypeStruct((tokens, feats), jnp.bfloat16),
        compiler_params=pltpu.CompilerParams(vmem_limit_bytes=VMEM_LIMIT),
        cost_estimate=pl.CostEstimate(
            flops=4 * tokens * hidden * feats,
            bytes_accessed=4 * (tokens * hidden + hidden * feats + tokens * feats),
            transcendentals=0,
        ),
        name="input_grad",
    )(row, *pieces, mean_weight, perturbed, sign)


def weight_kernel(n_slab, n_piece, scale, row_ref, *refs):
    n_grads = n_slab * n_piece
    grads, inputs, signs = refs[:n_grads], refs[n_grads:n_grads + n_slab], refs[n_grads + n_slab:n_grads + 2 * n_slab]
    noise_ref, mean_ref, sigma_ref, plain, signed = refs[n_grads + 2 * n_slab:]
    rows = grads[0].shape[1]

    @pl.when(pl.program_id(1) == 0)
    def _():
        for j in range(n_slab):
            for k in range(n_piece):
                start = pl.multiple_of((row_ref[0] ^ k) * rows, rows)
                value = inputs[j][pl.ds(start, rows), :]
                at = (j * n_piece + k) * rows
                plain[at:at + rows, :] = value
                signed[at:at + rows, :] = value * signs[j][pl.ds(start, rows), :]

    dims = (((0,), (0,)), ((), ()))
    grad = jnp.concatenate([g[0] for g in grads], axis=0)
    mean = lax.dot_general(grad, plain[...], dims, preferred_element_type=jnp.float32)
    mean_ref[...] = mean * scale
    grad = jnp.concatenate([g[1] for g in grads], axis=0)
    sigma = lax.dot_general(grad, signed[...], dims, preferred_element_type=jnp.float32)
    sigma_ref[...] = sigma * scale * noise_ref[...].astype(jnp.float32)


def weight_grads(row, pieces, inputs, signs, noise, scale):
    n_slab, n_piece = len(pieces), len(pieces[0])
    hidden, feats = noise.shape
    slab = inputs[0].shape[0]
    tokens = slab * n_slab
    rows = pieces[0][0].shape[1]
    width = feats if tokens <= 1280 else min(256, feats)
    tile = 256 if hidden % 256 == 0 else hidden
    grad_spec = pl.BlockSpec((2, rows, tile), lambda f, h, row: (0, 0, h))
    slab_spec = pl.BlockSpec((slab, width), lambda f, h, row: (0, f))
    out_spec = pl.BlockSpec((tile, width), lambda f, h, row: (h, f))
    return pl.pallas_call(
        functools.partial(weight_kernel, n_slab, n_piece, scale),
        grid_spec=pltpu.PrefetchScalarGridSpec(
            num_scalar_prefetch=1,
            grid=(feats // width, hidden // tile),
            in_specs=[grad_spec] * (n_slab * n_piece) + [slab_spec] * (2 * n_slab) + [out_spec],
            out_specs=[out_spec, out_spec],
            scratch_shapes=[
                pltpu.VMEM((tokens, width), jnp.bfloat16),
                pltpu.VMEM((tokens, width), jnp.bfloat16),
            ],
        ),
        out_shape=[jax.ShapeDtypeStruct((hidden, feats), jnp.float32)] * 2,
        compiler_params=pltpu.CompilerParams(vmem_limit_bytes=VMEM_LIMIT),
        cost_estimate=pl.CostEstimate(
            flops=4 * tokens * hidden * feats,
            bytes_accessed=4 * (tokens * hidden + tokens * feats) + 10 * hidden * feats,
            transcendentals=0,
        ),
        name="weight_grads",
    )(row, *[p for slab_pieces in pieces for p in slab_pieces], *inputs, *signs, noise)


def local(inputs, in_bits, out_grads, out_bits, mean_weight, sigma_weight, noise):
    n_depth, n_row = lax.axis_size("depth"), lax.axis_size("row")
    depth = lax.axis_index("depth")
    row = lax.axis_index("row").astype(jnp.int32).reshape(1)
    hidden = mean_weight.shape[0]
    tokens_total = inputs.shape[0] * lax.axis_size("col") * n_depth

    in_sign = (1 - 2 * in_bits).astype(jnp.bfloat16)
    signed_grads = out_grads * (1 - 2 * out_bits).astype(jnp.bfloat16)
    perturbed = (sigma_weight.astype(jnp.float32) * noise.astype(jnp.float32)).astype(jnp.bfloat16)

    def hop(value, step):
        pairs = [(i, (i + step) % n_depth) for i in range(n_depth)]
        return lax.ppermute(value, "depth", pairs)

    def swap(value, bit):
        return lax.ppermute(value, "row", [(i, i ^ bit) for i in range(n_row)])

    def half(step):
        start = ((depth + step) % n_depth) * hidden
        return jnp.stack([lax.dynamic_slice_in_dim(a, start, hidden, 1) for a in (out_grads, signed_grads)])

    slab_sign = [lax.all_gather(in_sign, "col", axis=0, tiled=True)]
    slab_inputs = [lax.all_gather(inputs, "col", axis=0, tiled=True)]
    pieces = []
    for j in range(n_depth):
        mine = half(j)
        if j:
            mine = hop(mine, j)
        slab_pieces = [mine]
        bit = 1
        while bit < n_row:
            slab_pieces += [None] * bit
            bit *= 2
        filled = [0]
        bit = n_row // 2
        while bit:
            for at in list(filled):
                slab_pieces[at ^ bit] = swap(slab_pieces[at], bit)
                filled.append(at ^ bit)
            bit //= 2
        pieces.append(slab_pieces)
    for j in range(1, n_depth):
        slab_sign.append(hop(slab_sign[0], j))
        slab_inputs.append(hop(slab_inputs[0], j))

    total = None
    for j in range(n_depth):
        part = partial_input_grad(row, pieces[j], mean_weight, perturbed, slab_sign[j])
        owned = lax.psum_scatter(part, "col", scatter_dimension=0, tiled=True)
        if j:
            owned = hop(owned, n_depth - j)
        owned = owned.astype(jnp.float32)
        total = owned if total is None else total + owned
    input_grad = total.astype(jnp.bfloat16)

    mean_grad, sigma_grad = weight_grads(
        row, pieces, slab_inputs, slab_sign, noise, tokens_total ** (-0.5)
    )
    return (input_grad, mean_grad, sigma_grad)


def solution(mesh):
    return jax.shard_map(
        local,
        mesh=mesh,
        in_specs=(
            P(("depth", "col"), "row"),
            P(("depth", "col"), "row"),
            P(("depth", "row"), "col"),
            P(("depth", "row"), "col"),
            P(("col", "depth"), "row"),
            P(("col", "depth"), "row"),
            P(("col", "depth"), "row"),
        ),
        out_specs=(
            P(("depth", "col"), "row"),
            P(("col", "depth"), "row"),
            P(("col", "depth"), "row"),
        ),
        check_vma=False,
    )
```

```python
import functools

import jax
import jax.numpy as jnp
from jax import lax
from jax.experimental import pallas as pl
from jax.experimental.pallas import tpu as pltpu
from jax.sharding import PartitionSpec as P

VMEM_LIMIT = 56 * 1024 * 1024


def grad_kernel(n_piece, turn_ref, *refs):
    pieces, (mean_ref, pert_ref, sign_ref, out_ref, both, sems) = refs[:n_piece], refs[n_piece:]

    @pl.when(pl.program_id(0) == 0)
    def _():
        copies = [
            pltpu.make_async_copy(pieces[k], both.at[turn_ref[0] ^ k], sems.at[k])
            for k in range(n_piece)
        ]
        for copy in copies:
            copy.start()
        for copy in copies:
            copy.wait()

    rows, hidden = both.shape[2:]
    grads = both[:, 0].reshape(n_piece * rows, hidden)
    signed = both[:, 1].reshape(n_piece * rows, hidden)
    part_a = jnp.dot(grads, mean_ref[...], preferred_element_type=jnp.float32)
    part_b = jnp.dot(signed, pert_ref[...], preferred_element_type=jnp.float32)
    for k in range(n_piece):
        at = slice(k * rows, (k + 1) * rows)
        sign = sign_ref[k].astype(jnp.float32)
        out_ref[k] = (part_a[at] + part_b[at] * sign).astype(out_ref.dtype)


def partial_input_grad(turn, pieces, mean_weight, perturbed, sign, weight):
    hidden, feats = mean_weight.shape
    n_piece = len(pieces)
    rows = sign.shape[1]
    tile = min(256, feats)
    any_spec = pl.BlockSpec(memory_space=pl.ANY)
    weight_spec = pl.BlockSpec((hidden, tile), lambda f, turn: (0, f))
    return pl.pallas_call(
        functools.partial(grad_kernel, n_piece),
        grid_spec=pltpu.PrefetchScalarGridSpec(
            num_scalar_prefetch=1,
            grid=(feats // tile,),
            in_specs=[any_spec] * n_piece
            + [weight_spec, weight_spec, pl.BlockSpec((n_piece, rows, tile), lambda f, turn: (0, 0, f))],
            out_specs=pl.BlockSpec((n_piece, rows, tile), lambda f, turn: (0, 0, f)),
            scratch_shapes=[
                pltpu.VMEM((n_piece,) + pieces[0].shape, jnp.bfloat16),
                pltpu.SemaphoreType.DMA((n_piece,)),
            ],
        ),
        out_shape=jax.ShapeDtypeStruct((n_piece, rows, feats), jnp.bfloat16),
        compiler_params=pltpu.CompilerParams(vmem_limit_bytes=VMEM_LIMIT),
        cost_estimate=pl.CostEstimate(
            flops=int(weight * n_piece * rows * hidden * feats),
            bytes_accessed=4 * (n_piece * rows * (hidden + feats) + hidden * feats),
            transcendentals=0,
        ),
        name="input_grad",
    )(turn, *pieces, mean_weight, perturbed, sign)


def weight_kernel(n_slab, n_piece, n_input, scale, turn_ref, *refs):
    n_grads = n_slab * n_piece
    grads, inputs, refs = refs[:n_grads], refs[n_grads:n_grads + n_input], refs[n_grads + n_input:]
    signs, noise_ref, (mean_ref, sigma_ref, plain, signed) = refs[:n_slab], refs[n_slab], refs[-4:]
    rows = grads[0].shape[1]

    @pl.when(pl.program_id(1) == 0)
    def _():
        blocks = [ref.at[at] for ref in inputs for at in range(ref.shape[0])]
        for i, block in enumerate(blocks):
            j, k = i // n_piece, i % n_piece
            to = pl.ds(pl.multiple_of((j * n_piece + (k ^ turn_ref[0])) * rows, rows), rows)
            value = block[...]
            plain[to, :] = value
            signed[to, :] = value * signs[j][k]

    dims = (((0,), (0,)), ((), ()))
    grad = jnp.concatenate([g[0] for g in grads], axis=0)
    mean = lax.dot_general(grad, plain[...], dims, preferred_element_type=jnp.float32)
    mean_ref[...] = mean * scale
    grad = jnp.concatenate([g[1] for g in grads], axis=0)
    sigma = lax.dot_general(grad, signed[...], dims, preferred_element_type=jnp.float32)
    sigma_ref[...] = sigma * scale * noise_ref[...].astype(jnp.float32)


def weight_grads(turn, pieces, inputs, signs, noise, scale, part, partial):
    n_slab, n_piece = len(pieces), len(pieces[0])
    hidden, feats = noise.shape
    rows = pieces[0][0].shape[1]
    tokens = n_slab * n_piece * rows
    width = feats if tokens <= 1280 else min(256, feats)
    tile = 256 if hidden % 256 == 0 else hidden
    cut = (hidden // tile + 1) // 2
    first, steps = (0, cut) if part == 0 else (cut, hidden // tile - cut)
    if not steps:
        return partial
    grad_spec = pl.BlockSpec((2, rows, tile), lambda f, h, turn: (0, 0, h + first))
    out_spec = pl.BlockSpec((tile, width), lambda f, h, turn: (h + first, f))
    operands = [p for slab_pieces in pieces for p in slab_pieces] + inputs + signs + [noise]
    return pl.pallas_call(
        functools.partial(weight_kernel, n_slab, n_piece, len(inputs), scale),
        grid_spec=pltpu.PrefetchScalarGridSpec(
            num_scalar_prefetch=1,
            grid=(feats // width, steps),
            in_specs=[grad_spec] * (n_slab * n_piece)
            + [pl.BlockSpec(x.shape[:2] + (width,), lambda f, h, turn: (0, 0, f)) for x in inputs + signs]
            + [out_spec]
            + [pl.BlockSpec(memory_space=pl.ANY)] * len(partial),
            out_specs=[out_spec, out_spec],
            scratch_shapes=[
                pltpu.VMEM((tokens, width), jnp.bfloat16),
                pltpu.VMEM((tokens, width), jnp.bfloat16),
            ],
        ),
        out_shape=[jax.ShapeDtypeStruct((hidden, feats), jnp.float32)] * 2,
        input_output_aliases={1 + len(operands) + i: i for i in range(len(partial))},
        compiler_params=pltpu.CompilerParams(vmem_limit_bytes=VMEM_LIMIT),
        cost_estimate=pl.CostEstimate(
            flops=4 * tokens * tile * steps * feats,
            bytes_accessed=4 * (tokens * tile * steps + tokens * feats) + 10 * tile * steps * feats,
            transcendentals=0,
        ),
        name="weight_grads",
    )(turn, *operands, *partial)


def local(inputs, in_bits, out_grads, out_bits, mean_weight, sigma_weight, noise):
    n_depth, n_row, n_col = (lax.axis_size(a) for a in ("depth", "row", "col"))
    depth, row, col = (lax.axis_index(a) for a in ("depth", "row", "col"))
    hidden = mean_weight.shape[0]
    scale = (inputs.shape[0] * n_col * n_depth) ** (-0.5)
    turn = (row ^ col).astype(jnp.int32).reshape(1)

    def hop(value, step):
        return lax.ppermute(value, "depth", [(i, (i + step) % n_depth) for i in range(n_depth)])

    def swap(value, bit):
        return lax.ppermute(value, "row", [(i, i ^ bit) for i in range(n_row)])

    def cross(value, bits):
        return lax.ppermute(value, "col", [(i, i ^ bits) for i in range(n_col)])

    def half(step):
        start = ((depth + step) % n_depth) * hidden
        return jnp.stack([lax.dynamic_slice_in_dim(a, start, hidden, 1) for a in (out_grads, signed_grads)])

    def tie(*values):
        return lax.optimization_barrier(values)

    signed_grads = out_grads * (1 - 2 * out_bits).astype(jnp.bfloat16)
    signed_grads, in_bits = tie(signed_grads, in_bits)
    in_sign = (1 - 2 * in_bits).astype(jnp.bfloat16)
    perturbed = (sigma_weight.astype(jnp.float32) * noise.astype(jnp.float32)).astype(jnp.bfloat16)

    mine = half(0)
    others = [hop(half(j), j) for j in range(1, n_depth)]
    signs = [in_sign, cross(in_sign, 1), None, cross(in_sign, 3)]
    signs[1], signs[3] = tie(signs[1], signs[3])
    signs[2] = cross(signs[3], 1)
    across, perturbed, signs[2] = tie(swap(mine, 2), perturbed, signs[2])
    pieces = [[mine, swap(mine, 1), across, swap(across, 1)]]
    pieces[0], others, signs, inputs = tie(pieces[0], others, jnp.stack(signs), inputs)

    own = partial_input_grad(turn, pieces[0], mean_weight, perturbed, signs, 64)
    blocks = [inputs, cross(inputs, 1), None, cross(inputs, 3)]
    blocks[1], blocks[3], own = tie(blocks[1], blocks[3], own)
    blocks[2] = cross(blocks[3], 1)
    passed = cross(own[2], 1)
    across = [swap(other, 2) for other in others]
    slab_sign = [signs] + [hop(signs, j) for j in range(1, n_depth)]
    across, slab_sign, blocks[2], passed = tie(across, slab_sign, blocks[2], passed)
    blocks = jnp.stack(blocks)

    def scatter(part, passed):
        joined = (part[3].astype(jnp.float32) + passed.astype(jnp.float32)).astype(jnp.bfloat16)
        return [part[0], cross(part[1], 1), cross(joined, 3)]

    owned = scatter(own, passed)
    slab_inputs = [blocks]
    total, grads = None, []
    for j in range(1, n_depth):
        hopped = hop(blocks, j)
        pieces.append([others[j - 1], swap(others[j - 1], 1), across[j - 1], swap(across[j - 1], 1)])
        part = partial_input_grad(turn, pieces[j], mean_weight, perturbed, slab_sign[j], 64)
        part, owned = tie(part, owned)
        if j == 1:
            total = sum(x.astype(jnp.float32) for x in owned)
        parts = scatter(part, cross(part[2], 1))
        parts[0], hopped = tie(parts[0], hopped)
        slab_inputs.append(hopped)
        if j == n_depth - 1:
            grads = weight_grads(turn, pieces, slab_inputs, slab_sign, noise, scale, 0, [])
            parts, grads = tie(parts, grads)
        part = sum(x.astype(jnp.float32) for x in parts).astype(jnp.bfloat16)
        total += hop(part, n_depth - j).astype(jnp.float32)
    input_grad = total.astype(jnp.bfloat16)
    grads = weight_grads(turn, pieces, slab_inputs, slab_sign, noise, scale, 1, grads)
    mean_grad, sigma_grad = grads
    return (input_grad, mean_grad, sigma_grad)


def solution(mesh):
    return jax.shard_map(
        local,
        mesh=mesh,
        in_specs=(
            P(("depth", "col"), "row"),
            P(("depth", "col"), "row"),
            P(("depth", "row"), "col"),
            P(("depth", "row"), "col"),
            P(("col", "depth"), "row"),
            P(("col", "depth"), "row"),
            P(("col", "depth"), "row"),
        ),
        out_specs=(
            P(("depth", "col"), "row"),
            P(("col", "depth"), "row"),
            P(("col", "depth"), "row"),
        ),
        check_vma=False,
    )
```

```python
import functools

import jax
import jax.numpy as jnp
from jax import lax
from jax.experimental import pallas as pl
from jax.experimental.pallas import tpu as pltpu
from jax.sharding import PartitionSpec as P

VMEM_LIMIT = 34 * 1024 * 1024
VMEM_LIMIT_GRAD = 18 * 1024 * 1024
ORDER = (0, 1, 3, 2)


def grad_kernel(n_piece, turn_ref, *refs):
    pieces, (mean_ref, pert_ref, head_ref, tail_ref) = refs[:n_piece], refs[n_piece:n_piece + 4]
    outs, (both, sems) = refs[n_piece + 4:-2], refs[-2:]

    @pl.when(pl.program_id(0) == 0)
    def _():
        copies = [
            pltpu.make_async_copy(pieces[k], both.at[turn_ref[0] ^ k], sems.at[k])
            for k in range(n_piece)
        ]
        for copy in copies:
            copy.start()
        for copy in copies:
            copy.wait()

    rows, hidden = both.shape[2:]
    grads = both[:, 0].reshape(n_piece * rows, hidden)
    signed = both[:, 1].reshape(n_piece * rows, hidden)
    part_a = jnp.dot(grads, mean_ref[...], preferred_element_type=jnp.float32)
    part_b = jnp.dot(signed, pert_ref[...], preferred_element_type=jnp.float32)
    for k in range(n_piece):
        at = slice(k * rows, (k + 1) * rows)
        block = ORDER.index(k)
        sign = (head_ref[block] if block < n_piece - 1 else tail_ref[...]).astype(jnp.float32)
        outs[k][...] = (part_a[at] + part_b[at] * sign).astype(outs[k].dtype)


def partial_input_grad(turn, pieces, mean_weight, perturbed, signs, weight):
    hidden, feats = mean_weight.shape
    n_piece, rows = len(pieces), pieces[0].shape[1]
    tile = min(256, feats)
    any_spec = pl.BlockSpec(memory_space=pl.ANY)
    weight_spec = pl.BlockSpec((hidden, tile), lambda f, turn: (0, f))
    block_spec = pl.BlockSpec((rows, tile), lambda f, turn: (0, f))
    return pl.pallas_call(
        functools.partial(grad_kernel, n_piece),
        grid_spec=pltpu.PrefetchScalarGridSpec(
            num_scalar_prefetch=1,
            grid=(feats // tile,),
            in_specs=[any_spec] * n_piece
            + [weight_spec, weight_spec, pl.BlockSpec((n_piece - 1, rows, tile), lambda f, turn: (0, 0, f)), block_spec],
            out_specs=[block_spec] * n_piece,
            scratch_shapes=[
                pltpu.VMEM((n_piece,) + pieces[0].shape, jnp.bfloat16),
                pltpu.SemaphoreType.DMA((n_piece,)),
            ],
        ),
        out_shape=[jax.ShapeDtypeStruct((rows, feats), jnp.bfloat16)] * n_piece,
        compiler_params=pltpu.CompilerParams(vmem_limit_bytes=VMEM_LIMIT_GRAD),
        cost_estimate=pl.CostEstimate(
            flops=int(weight * n_piece * rows * hidden * feats),
            bytes_accessed=4 * (n_piece * rows * (hidden + feats) + hidden * feats),
            transcendentals=0,
        ),
        name="input_grad",
    )(turn, *pieces, mean_weight, perturbed, *signs)


def weight_kernel(n_slab, n_piece, scale, turn_ref, *refs):
    n_grads = n_slab * n_piece
    grads, inputs, signs = refs[:n_grads], refs[n_grads:n_grads + 2 * n_slab], refs[n_grads + 2 * n_slab:n_grads + 4 * n_slab]
    noise_ref, (mean_ref, sigma_ref, plain, signed) = refs[n_grads + 4 * n_slab], refs[-4:]
    rows = grads[0].shape[1]

    @pl.when(pl.program_id(1) == 0)
    def _():
        for j in range(n_slab):
            for i, k in enumerate(ORDER):
                to = pl.ds(pl.multiple_of((j * n_piece + (k ^ turn_ref[0])) * rows, rows), rows)
                value, sign = (
                    group[2 * j][i] if i < n_piece - 1 else group[2 * j + 1][...] for group in (inputs, signs)
                )
                plain[to, :] = value
                signed[to, :] = value * sign

    dims = (((0,), (0,)), ((), ()))
    grad = jnp.concatenate([g[0] for g in grads], axis=0)
    mean = lax.dot_general(grad, plain[...], dims, preferred_element_type=jnp.float32)
    mean_ref[...] = mean * scale
    grad = jnp.concatenate([g[1] for g in grads], axis=0)
    sigma = lax.dot_general(grad, signed[...], dims, preferred_element_type=jnp.float32)
    sigma_ref[...] = sigma * scale * noise_ref[...].astype(jnp.float32)


def weight_grads(turn, pieces, inputs, signs, noise, scale, part, partial):
    n_slab, n_piece = len(pieces), len(pieces[0])
    hidden, feats = noise.shape
    rows = pieces[0][0].shape[1]
    tokens = n_slab * n_piece * rows
    width = feats if tokens <= 1280 else min(256, feats)
    tile = 256 if hidden % 256 == 0 else hidden
    cut = (hidden // tile + 1) // 2
    first, steps = (0, cut) if part == 0 else (cut, hidden // tile - cut)
    if not steps:
        return partial
    grad_spec = pl.BlockSpec((2, rows, tile), lambda f, h, turn: (0, 0, h + first))
    out_spec = pl.BlockSpec((tile, width), lambda f, h, turn: (h + first, f))
    inputs, signs = ([x for slab in group for x in slab] for group in (inputs, signs))
    operands = [p for slab_pieces in pieces for p in slab_pieces] + inputs + signs + [noise]
    return pl.pallas_call(
        functools.partial(weight_kernel, n_slab, n_piece, scale),
        grid_spec=pltpu.PrefetchScalarGridSpec(
            num_scalar_prefetch=1,
            grid=(feats // width, steps),
            in_specs=[grad_spec] * (n_slab * n_piece)
            + [
                pl.BlockSpec(x.shape[:-1] + (width,), lambda f, h, turn, lead=x.ndim - 1: (0,) * lead + (f,))
                for x in inputs + signs
            ]
            + [out_spec]
            + [pl.BlockSpec(memory_space=pl.ANY)] * len(partial),
            out_specs=[out_spec, out_spec],
            scratch_shapes=[
                pltpu.VMEM((tokens, width), jnp.bfloat16),
                pltpu.VMEM((tokens, width), jnp.bfloat16),
            ],
        ),
        out_shape=[jax.ShapeDtypeStruct((hidden, feats), jnp.float32)] * 2,
        input_output_aliases={1 + len(operands) + i: i for i in range(len(partial))},
        compiler_params=pltpu.CompilerParams(vmem_limit_bytes=VMEM_LIMIT),
        cost_estimate=pl.CostEstimate(
            flops=4 * tokens * tile * steps * feats if part else 1,
            bytes_accessed=4 * (tokens * tile * steps + tokens * feats) + 10 * tile * steps * feats if part else 1,
            transcendentals=0,
        ),
        name="weight_grads",
    )(turn, *operands, *partial)


def local(inputs, in_bits, out_grads, out_bits, mean_weight, sigma_weight, noise):
    n_depth, n_row, n_col = (lax.axis_size(a) for a in ("depth", "row", "col"))
    depth, row, col = (lax.axis_index(a) for a in ("depth", "row", "col"))
    hidden = mean_weight.shape[0]
    scale = (inputs.shape[0] * n_col * n_depth) ** (-0.5)
    turn = (row ^ col).astype(jnp.int32).reshape(1)

    def hop(value, step):
        return lax.ppermute(value, "depth", [(i, (i + step) % n_depth) for i in range(n_depth)])

    def swap(value, bit):
        return lax.ppermute(value, "row", [(i, i ^ bit) for i in range(n_row)])

    def cross(value, bits):
        return lax.ppermute(value, "col", [(i, i ^ bits) for i in range(n_col)])

    def half(step):
        start = ((depth + step) % n_depth) * hidden
        return jnp.stack([lax.dynamic_slice_in_dim(a, start, hidden, 1) for a in (out_grads, signed_grads)])

    def tie(*values):
        return lax.optimization_barrier(values)

    signed_grads = out_grads * (1 - 2 * out_bits).astype(jnp.bfloat16)
    mine, others = half(0), [half(j) for j in range(1, n_depth)]
    others, in_bits = tie(others, in_bits)
    in_sign = (1 - 2 * in_bits).astype(jnp.bfloat16)
    perturbed = (sigma_weight.astype(jnp.float32) * noise.astype(jnp.float32)).astype(jnp.bfloat16)

    others = [hop(other, j + 1) for j, other in enumerate(others)]
    signs = [in_sign, cross(in_sign, 1), None, cross(in_sign, 3)]
    signs[1], signs[3] = tie(signs[1], signs[3])
    signs[2] = cross(signs[3], 1)
    across, others, perturbed, signs, inputs = tie(swap(mine, 2), others, perturbed, signs, inputs)
    head, tail = jnp.stack([signs[0], signs[1], signs[3]]), signs[2]
    pieces = [[mine, swap(mine, 1), across, swap(across, 1)]]

    slab_sign = [[head, tail]] + [[hop(head, j), hop(tail, j)] for j in range(1, n_depth)]
    own = partial_input_grad(turn, pieces[0], mean_weight, perturbed, slab_sign[0], 64)
    blocks = [inputs, cross(inputs, 1), None, cross(inputs, 3)]
    blocks[1], blocks[3], own = tie(blocks[1], blocks[3], own)
    blocks[2] = cross(blocks[3], 1)
    passed = cross(own[2], 1)
    across = [swap(other, 2) for other in others]
    across, slab_sign, blocks[2], passed = tie(across, slab_sign, blocks[2], passed)
    blocks = [jnp.stack([blocks[0], blocks[1], blocks[3]]), blocks[2]]

    def scatter(part, passed):
        joined = (part[3].astype(jnp.float32) + passed.astype(jnp.float32)).astype(jnp.bfloat16)
        return [part[0], cross(part[1], 1), cross(joined, 3)]

    owned = scatter(own, passed)
    slab_inputs = [blocks]
    total, grads = None, []
    for j in range(1, n_depth):
        hopped = [hop(x, j) for x in blocks]
        pieces.append([others[j - 1], swap(others[j - 1], 1), across[j - 1], swap(across[j - 1], 1)])
        part = partial_input_grad(turn, pieces[j], mean_weight, perturbed, slab_sign[j], 4)
        passed = cross(part[2], 1)
        if j == 1:
            passed, owned = tie(passed, owned)
            total = sum(x.astype(jnp.float32) for x in owned)
        parts = scatter(part, passed)
        parts[0], hopped = tie(parts[0], hopped)
        slab_inputs.append(hopped)
        if j == n_depth - 1:
            grads = weight_grads(turn, pieces, slab_inputs, slab_sign, noise, scale, 0, [])
            parts, grads = tie(parts, grads)
        part = sum(x.astype(jnp.float32) for x in parts).astype(jnp.bfloat16)
        total += hop(part, n_depth - j).astype(jnp.float32)
    input_grad = total.astype(jnp.bfloat16)
    grads = weight_grads(turn, pieces, slab_inputs, slab_sign, noise, scale, 1, grads)
    mean_grad, sigma_grad = grads
    return (input_grad, mean_grad, sigma_grad)


def solution(mesh):
    return jax.shard_map(
        local,
        mesh=mesh,
        in_specs=(
            P(("depth", "col"), "row"),
            P(("depth", "col"), "row"),
            P(("depth", "row"), "col"),
            P(("depth", "row"), "col"),
            P(("col", "depth"), "row"),
            P(("col", "depth"), "row"),
            P(("col", "depth"), "row"),
        ),
        out_specs=(
            P(("depth", "col"), "row"),
            P(("col", "depth"), "row"),
            P(("col", "depth"), "row"),
        ),
        check_vma=False,
    )
```

```python
import functools

import jax
import jax.numpy as jnp
from jax import lax
from jax.experimental import pallas as pl
from jax.experimental.pallas import tpu as pltpu
from jax.sharding import PartitionSpec as P

VMEM_LIMIT = 34 * 1024 * 1024
VMEM_LIMIT_GRAD = 18 * 1024 * 1024
OWN_LIMIT = 50 * 1024 * 1024
ORDER = (0, 1, 3, 2)


def grad_kernel(n_piece, turn_ref, *refs):
    pieces, (mean_ref, pert_ref, head_ref, tail_ref) = refs[:n_piece], refs[n_piece:n_piece + 4]
    outs, (both, sems) = refs[n_piece + 4:-2], refs[-2:]

    @pl.when(pl.program_id(0) == 0)
    def _():
        copies = [
            pltpu.make_async_copy(pieces[k], both.at[turn_ref[0] ^ k], sems.at[k])
            for k in range(n_piece)
        ]
        for copy in copies:
            copy.start()
        for copy in copies:
            copy.wait()

    rows, hidden = both.shape[2:]
    grads = both[:, 0].reshape(n_piece * rows, hidden)
    signed = both[:, 1].reshape(n_piece * rows, hidden)
    part_a = jnp.dot(grads, mean_ref[...], preferred_element_type=jnp.float32)
    part_b = jnp.dot(signed, pert_ref[...], preferred_element_type=jnp.float32)
    for k in range(n_piece):
        at = slice(k * rows, (k + 1) * rows)
        block = ORDER.index(k)
        sign = (head_ref[block] if block < n_piece - 1 else tail_ref[...]).astype(jnp.float32)
        outs[k][...] = (part_a[at] + part_b[at] * sign).astype(outs[k].dtype)


def partial_input_grad(turn, pieces, mean_weight, perturbed, signs, weight, limit):
    hidden, feats = mean_weight.shape
    n_piece, rows = len(pieces), pieces[0].shape[1]
    tile = min(256, feats)
    any_spec = pl.BlockSpec(memory_space=pl.ANY)
    weight_spec = pl.BlockSpec((hidden, tile), lambda f, turn: (0, f))
    block_spec = pl.BlockSpec((rows, tile), lambda f, turn: (0, f))
    return pl.pallas_call(
        functools.partial(grad_kernel, n_piece),
        grid_spec=pltpu.PrefetchScalarGridSpec(
            num_scalar_prefetch=1,
            grid=(feats // tile,),
            in_specs=[any_spec] * n_piece
            + [weight_spec, weight_spec, pl.BlockSpec((n_piece - 1, rows, tile), lambda f, turn: (0, 0, f)), block_spec],
            out_specs=[block_spec] * n_piece,
            scratch_shapes=[
                pltpu.VMEM((n_piece,) + pieces[0].shape, jnp.bfloat16),
                pltpu.SemaphoreType.DMA((n_piece,)),
            ],
        ),
        out_shape=[jax.ShapeDtypeStruct((rows, feats), jnp.bfloat16)] * n_piece,
        compiler_params=pltpu.CompilerParams(vmem_limit_bytes=limit),
        cost_estimate=pl.CostEstimate(
            flops=int(weight * n_piece * rows * hidden * feats),
            bytes_accessed=4 * (n_piece * rows * (hidden + feats) + hidden * feats),
            transcendentals=0,
        ),
        name="input_grad",
    )(turn, *pieces, mean_weight, perturbed, *signs)


def weight_kernel(n_slab, n_piece, scale, turn_ref, *refs):
    n_grads = n_slab * n_piece
    grads, inputs, signs = refs[:n_grads], refs[n_grads:n_grads + 2 * n_slab], refs[n_grads + 2 * n_slab:n_grads + 4 * n_slab]
    noise_ref, (mean_ref, sigma_ref, plain, signed) = refs[n_grads + 4 * n_slab], refs[-4:]
    rows = grads[0].shape[1]

    @pl.when(pl.program_id(1) == 0)
    def _():
        for j in range(n_slab):
            for i, k in enumerate(ORDER):
                to = pl.ds(pl.multiple_of((j * n_piece + (k ^ turn_ref[0])) * rows, rows), rows)
                value, sign = (
                    group[2 * j][i] if i < n_piece - 1 else group[2 * j + 1][...] for group in (inputs, signs)
                )
                plain[to, :] = value
                signed[to, :] = value * sign

    dims = (((0,), (0,)), ((), ()))
    grad = jnp.concatenate([g[0] for g in grads], axis=0)
    mean = lax.dot_general(grad, plain[...], dims, preferred_element_type=jnp.float32)
    mean_ref[...] = mean * scale
    grad = jnp.concatenate([g[1] for g in grads], axis=0)
    sigma = lax.dot_general(grad, signed[...], dims, preferred_element_type=jnp.float32)
    sigma_ref[...] = sigma * scale * noise_ref[...].astype(jnp.float32)


def weight_grads(turn, pieces, inputs, signs, noise, scale, part, partial):
    n_slab, n_piece = len(pieces), len(pieces[0])
    hidden, feats = noise.shape
    rows = pieces[0][0].shape[1]
    tokens = n_slab * n_piece * rows
    width = feats if tokens <= 1280 else min(256, feats)
    tile = 256 if hidden % 256 == 0 else hidden
    cut = (hidden // tile + 1) // 2
    first, steps = (0, cut) if part == 0 else (cut, hidden // tile - cut)
    if not steps:
        return partial
    grad_spec = pl.BlockSpec((2, rows, tile), lambda f, h, turn: (0, 0, h + first))
    out_spec = pl.BlockSpec((tile, width), lambda f, h, turn: (h + first, f))
    inputs, signs = ([x for slab in group for x in slab] for group in (inputs, signs))
    operands = [p for slab_pieces in pieces for p in slab_pieces] + inputs + signs + [noise]
    return pl.pallas_call(
        functools.partial(weight_kernel, n_slab, n_piece, scale),
        grid_spec=pltpu.PrefetchScalarGridSpec(
            num_scalar_prefetch=1,
            grid=(feats // width, steps),
            in_specs=[grad_spec] * (n_slab * n_piece)
            + [
                pl.BlockSpec(x.shape[:-1] + (width,), lambda f, h, turn, lead=x.ndim - 1: (0,) * lead + (f,))
                for x in inputs + signs
            ]
            + [out_spec]
            + [pl.BlockSpec(memory_space=pl.ANY)] * len(partial),
            out_specs=[out_spec, out_spec],
            scratch_shapes=[
                pltpu.VMEM((tokens, width), jnp.bfloat16),
                pltpu.VMEM((tokens, width), jnp.bfloat16),
            ],
        ),
        out_shape=[jax.ShapeDtypeStruct((hidden, feats), jnp.float32)] * 2,
        input_output_aliases={1 + len(operands) + i: i for i in range(len(partial))},
        compiler_params=pltpu.CompilerParams(vmem_limit_bytes=VMEM_LIMIT),
        cost_estimate=pl.CostEstimate(
            flops=4 * tokens * tile * steps * feats if part else 1,
            bytes_accessed=4 * (tokens * tile * steps + tokens * feats) + 10 * tile * steps * feats if part else 1,
            transcendentals=0,
        ),
        name="weight_grads",
    )(turn, *operands, *partial)


def local(inputs, in_bits, out_grads, out_bits, mean_weight, sigma_weight, noise):
    n_depth, n_row, n_col = (lax.axis_size(a) for a in ("depth", "row", "col"))
    depth, row, col = (lax.axis_index(a) for a in ("depth", "row", "col"))
    hidden = mean_weight.shape[0]
    scale = (inputs.shape[0] * n_col * n_depth) ** (-0.5)
    turn = (row ^ col).astype(jnp.int32).reshape(1)

    def hop(value, step):
        return lax.ppermute(value, "depth", [(i, (i + step) % n_depth) for i in range(n_depth)])

    def swap(value, bit):
        return lax.ppermute(value, "row", [(i, i ^ bit) for i in range(n_row)])

    def cross(value, bits):
        return lax.ppermute(value, "col", [(i, i ^ bits) for i in range(n_col)])

    def half(step):
        start = ((depth + step) % n_depth) * hidden
        grads, bits = (lax.dynamic_slice_in_dim(a, start, hidden, 1) for a in (out_grads, out_bits))
        return jnp.stack([grads, grads * (1 - 2 * bits).astype(jnp.bfloat16)])

    def tie(*values):
        return lax.optimization_barrier(values)

    mine, others = half(0), [half(j) for j in range(1, n_depth)]
    others, in_bits = tie(others, in_bits)
    in_sign = (1 - 2 * in_bits).astype(jnp.bfloat16)
    perturbed = (sigma_weight.astype(jnp.float32) * noise.astype(jnp.float32)).astype(jnp.bfloat16)

    others = [hop(other, j + 1) for j, other in enumerate(others)]
    signs = [in_sign, cross(in_sign, 1), None, cross(in_sign, 3)]
    signs[1], signs[3] = tie(signs[1], signs[3])
    signs[2] = cross(signs[3], 1)
    across, others, perturbed, signs, inputs = tie(swap(mine, 2), others, perturbed, signs, inputs)
    head, tail = jnp.stack([signs[0], signs[1], signs[3]]), signs[2]
    pieces = [[mine, swap(mine, 1), across, swap(across, 1)]]

    slab_sign = [[head, tail]] + [[hop(head, j), hop(tail, j)] for j in range(1, n_depth)]
    own = partial_input_grad(turn, pieces[0], mean_weight, perturbed, slab_sign[0], 64, OWN_LIMIT)
    blocks = [inputs, cross(inputs, 1), None, cross(inputs, 3)]
    blocks[1], blocks[3], own = tie(blocks[1], blocks[3], own)
    blocks[2] = cross(blocks[3], 1)
    passed = cross(own[2], 1)
    across = [swap(other, 2) for other in others]
    across, slab_sign, blocks[2], passed = tie(across, slab_sign, blocks[2], passed)
    blocks = [jnp.stack([blocks[0], blocks[1], blocks[3]]), blocks[2]]

    def scatter(part, passed):
        joined = (part[3].astype(jnp.float32) + passed.astype(jnp.float32)).astype(jnp.bfloat16)
        return [part[0], cross(part[1], 1), cross(joined, 3)]

    owned = scatter(own, passed)
    slab_inputs = [blocks]
    total, grads = None, []
    for j in range(1, n_depth):
        hopped = [hop(x, j) for x in blocks]
        pieces.append([others[j - 1], swap(others[j - 1], 1), across[j - 1], swap(across[j - 1], 1)])
        part = partial_input_grad(turn, pieces[j], mean_weight, perturbed, slab_sign[j], 4, VMEM_LIMIT_GRAD)
        passed = cross(part[2], 1)
        if j == 1:
            passed, owned = tie(passed, owned)
            total = sum(x.astype(jnp.float32) for x in owned)
        parts = scatter(part, passed)
        parts[0], hopped = tie(parts[0], hopped)
        slab_inputs.append(hopped)
        if j == n_depth - 1:
            grads = weight_grads(turn, pieces, slab_inputs, slab_sign, noise, scale, 0, [])
            parts, grads = tie(parts, grads)
        part = sum(x.astype(jnp.float32) for x in parts).astype(jnp.bfloat16)
        total += hop(part, n_depth - j).astype(jnp.float32)
    input_grad = total.astype(jnp.bfloat16)
    grads = weight_grads(turn, pieces, slab_inputs, slab_sign, noise, scale, 1, grads)
    mean_grad, sigma_grad = grads
    return (input_grad, mean_grad, sigma_grad)


def solution(mesh):
    return jax.shard_map(
        local,
        mesh=mesh,
        in_specs=(
            P(("depth", "col"), "row"),
            P(("depth", "col"), "row"),
            P(("depth", "row"), "col"),
            P(("depth", "row"), "col"),
            P(("col", "depth"), "row"),
            P(("col", "depth"), "row"),
            P(("col", "depth"), "row"),
        ),
        out_specs=(
            P(("depth", "col"), "row"),
            P(("col", "depth"), "row"),
            P(("col", "depth"), "row"),
        ),
        check_vma=False,
    )
```

```python
import functools

import jax
import jax.numpy as jnp
from jax import lax
from jax.experimental import pallas as pl
from jax.experimental.pallas import tpu as pltpu
from jax.sharding import PartitionSpec as P

VMEM_LIMIT = 34 * 1024 * 1024
VMEM_LIMIT_GRAD = 18 * 1024 * 1024
OWN_LIMIT = 50 * 1024 * 1024
ORDER = (0, 1, 3, 2)


def grad_kernel(n_piece, turn_ref, *refs):
    pieces, (mean_ref, pert_ref, head_ref, tail_ref) = refs[:n_piece], refs[n_piece:n_piece + 4]
    outs, (both, sems) = refs[n_piece + 4:-2], refs[-2:]

    @pl.when(pl.program_id(0) == 0)
    def _():
        copies = [
            pltpu.make_async_copy(pieces[k], both.at[turn_ref[0] ^ k], sems.at[k])
            for k in range(n_piece)
        ]
        for copy in copies:
            copy.start()
        for copy in copies:
            copy.wait()

    rows, hidden = both.shape[2:]
    grads = both[:, 0].reshape(n_piece * rows, hidden)
    signed = both[:, 1].reshape(n_piece * rows, hidden)
    part_a = jnp.dot(grads, mean_ref[...], preferred_element_type=jnp.float32)
    part_b = jnp.dot(signed, pert_ref[...], preferred_element_type=jnp.float32)
    for k in range(n_piece):
        at = slice(k * rows, (k + 1) * rows)
        block = ORDER.index(k)
        sign = (head_ref[block] if block < n_piece - 1 else tail_ref[...]).astype(jnp.float32)
        outs[k][...] = (part_a[at] + part_b[at] * sign).astype(outs[k].dtype)


def partial_input_grad(turn, pieces, mean_weight, perturbed, signs, weight, limit):
    hidden, feats = mean_weight.shape
    n_piece, rows = len(pieces), pieces[0].shape[1]
    tile = min(256, feats)
    any_spec = pl.BlockSpec(memory_space=pl.ANY)
    weight_spec = pl.BlockSpec((hidden, tile), lambda f, turn: (0, f))
    block_spec = pl.BlockSpec((rows, tile), lambda f, turn: (0, f))
    return pl.pallas_call(
        functools.partial(grad_kernel, n_piece),
        grid_spec=pltpu.PrefetchScalarGridSpec(
            num_scalar_prefetch=1,
            grid=(feats // tile,),
            in_specs=[any_spec] * n_piece
            + [weight_spec, weight_spec, pl.BlockSpec((n_piece - 1, rows, tile), lambda f, turn: (0, 0, f)), block_spec],
            out_specs=[block_spec] * n_piece,
            scratch_shapes=[
                pltpu.VMEM((n_piece,) + pieces[0].shape, jnp.bfloat16),
                pltpu.SemaphoreType.DMA((n_piece,)),
            ],
        ),
        out_shape=[jax.ShapeDtypeStruct((rows, feats), jnp.bfloat16)] * n_piece,
        compiler_params=pltpu.CompilerParams(vmem_limit_bytes=limit),
        cost_estimate=pl.CostEstimate(
            flops=int(weight * n_piece * rows * hidden * feats),
            bytes_accessed=4 * (n_piece * rows * (hidden + feats) + hidden * feats),
            transcendentals=0,
        ),
        name="input_grad",
    )(turn, *pieces, mean_weight, perturbed, *signs)


def weight_kernel(n_slab, n_piece, scale, turn_ref, *refs):
    n_grads = n_slab * n_piece
    grads, inputs, signs = refs[:n_grads], refs[n_grads:n_grads + 2 * n_slab], refs[n_grads + 2 * n_slab:n_grads + 4 * n_slab]
    noise_ref, (mean_ref, sigma_ref, plain, signed) = refs[n_grads + 4 * n_slab], refs[-4:]
    rows = grads[0].shape[1]

    @pl.when(pl.program_id(1) == 0)
    def _():
        for j in range(n_slab):
            for i, k in enumerate(ORDER):
                to = pl.ds(pl.multiple_of((j * n_piece + (k ^ turn_ref[0])) * rows, rows), rows)
                value, sign = (
                    group[2 * j][i] if i < n_piece - 1 else group[2 * j + 1][...] for group in (inputs, signs)
                )
                plain[to, :] = value
                signed[to, :] = value * sign

    dims = (((0,), (0,)), ((), ()))
    grad = jnp.concatenate([g[0] for g in grads], axis=0)
    mean = lax.dot_general(grad, plain[...], dims, preferred_element_type=jnp.float32)
    mean_ref[...] = mean * scale
    grad = jnp.concatenate([g[1] for g in grads], axis=0)
    sigma = lax.dot_general(grad, signed[...], dims, preferred_element_type=jnp.float32)
    sigma_ref[...] = sigma * scale * noise_ref[...].astype(jnp.float32)


def weight_grads(turn, pieces, inputs, signs, noise, scale, part, partial):
    n_slab, n_piece = len(pieces), len(pieces[0])
    hidden, feats = noise.shape
    rows = pieces[0][0].shape[1]
    tokens = n_slab * n_piece * rows
    width = feats if tokens <= 1280 else min(256, feats)
    tile = 256 if hidden % 256 == 0 else hidden
    cut = (hidden // tile + 1) // 2
    first, steps = (0, cut) if part == 0 else (cut, hidden // tile - cut)
    if not steps:
        return partial
    grad_spec = pl.BlockSpec((2, rows, tile), lambda f, h, turn: (0, 0, h + first))
    out_spec = pl.BlockSpec((tile, width), lambda f, h, turn: (h + first, f))
    inputs, signs = ([x for slab in group for x in slab] for group in (inputs, signs))
    operands = [p for slab_pieces in pieces for p in slab_pieces] + inputs + signs + [noise]
    return pl.pallas_call(
        functools.partial(weight_kernel, n_slab, n_piece, scale),
        grid_spec=pltpu.PrefetchScalarGridSpec(
            num_scalar_prefetch=1,
            grid=(feats // width, steps),
            in_specs=[grad_spec] * (n_slab * n_piece)
            + [
                pl.BlockSpec(x.shape[:-1] + (width,), lambda f, h, turn, lead=x.ndim - 1: (0,) * lead + (f,))
                for x in inputs + signs
            ]
            + [out_spec]
            + [pl.BlockSpec(memory_space=pl.ANY)] * len(partial),
            out_specs=[out_spec, out_spec],
            scratch_shapes=[
                pltpu.VMEM((tokens, width), jnp.bfloat16),
                pltpu.VMEM((tokens, width), jnp.bfloat16),
            ],
        ),
        out_shape=[jax.ShapeDtypeStruct((hidden, feats), jnp.float32)] * 2,
        input_output_aliases={1 + len(operands) + i: i for i in range(len(partial))},
        compiler_params=pltpu.CompilerParams(vmem_limit_bytes=VMEM_LIMIT),
        cost_estimate=pl.CostEstimate(
            flops=4 * tokens * tile * steps * feats if part else 1,
            bytes_accessed=4 * (tokens * tile * steps + tokens * feats) + 10 * tile * steps * feats if part else 1,
            transcendentals=0,
        ),
        name="weight_grads",
    )(turn, *operands, *partial)


def local(inputs, in_bits, out_grads, out_bits, mean_weight, sigma_weight, noise):
    n_depth, n_row, n_col = (lax.axis_size(a) for a in ("depth", "row", "col"))
    depth, row, col = (lax.axis_index(a) for a in ("depth", "row", "col"))
    hidden = mean_weight.shape[0]
    scale = (inputs.shape[0] * n_col * n_depth) ** (-0.5)
    turn = (row ^ col).astype(jnp.int32).reshape(1)

    def hop(value, step):
        return lax.ppermute(value, "depth", [(i, (i + step) % n_depth) for i in range(n_depth)])

    def swap(value, bit):
        return lax.ppermute(value, "row", [(i, i ^ bit) for i in range(n_row)])

    def cross(value, bits):
        return lax.ppermute(value, "col", [(i, i ^ bits) for i in range(n_col)])

    def half(step):
        start = ((depth + step) % n_depth) * hidden
        grads, bits = (lax.dynamic_slice_in_dim(a, start, hidden, 1) for a in (out_grads, out_bits))
        return jnp.stack([grads, grads * (1 - 2 * bits).astype(jnp.bfloat16)])

    def tie(*values):
        return lax.optimization_barrier(values)

    mine, others = half(0), [half(j) for j in range(1, n_depth)]
    others, in_bits = tie(others, in_bits)
    in_sign = (1 - 2 * in_bits).astype(jnp.bfloat16)
    perturbed = (sigma_weight.astype(jnp.float32) * noise.astype(jnp.float32)).astype(jnp.bfloat16)

    others = [hop(other, j + 1) for j, other in enumerate(others)]
    signs = [in_sign, cross(in_sign, 1), None, cross(in_sign, 3)]
    signs[1], signs[3] = tie(signs[1], signs[3])
    signs[2] = cross(signs[3], 1)
    across, others, perturbed, signs, inputs = tie(swap(mine, 2), others, perturbed, signs, inputs)
    head, tail = jnp.stack([signs[0], signs[1], signs[3]]), signs[2]
    head, late_inputs = tie(head, inputs)
    pieces = [[mine, swap(mine, 1), across, swap(across, 1)]]

    slab_sign = [[head, tail]] + [[hop(head, j), hop(tail, j)] for j in range(1, n_depth)]
    own = partial_input_grad(turn, pieces[0], mean_weight, perturbed, slab_sign[0], 64, OWN_LIMIT)
    blocks = [inputs, cross(inputs, 1), None, cross(late_inputs, 3)]
    blocks[1], own = tie(blocks[1], own)
    passed = cross(own[2], 1)
    across = [swap(other, 2) for other in others]
    across, slab_sign, blocks[1], blocks[3], passed = tie(across, slab_sign, blocks[1], blocks[3], passed)
    three, blocks[3] = tie(jnp.stack([blocks[0], blocks[1], blocks[3]]), blocks[3])
    blocks = [three, cross(blocks[3], 1)]

    def scatter(part, passed):
        joined = (part[3].astype(jnp.float32) + passed.astype(jnp.float32)).astype(jnp.bfloat16)
        return [part[0], cross(part[1], 1), cross(joined, 3)]

    owned = scatter(own, passed)
    slab_inputs = [blocks]
    total, grads = None, []
    for j in range(1, n_depth):
        hopped = [hop(x, j) for x in blocks]
        pieces.append([others[j - 1], swap(others[j - 1], 1), across[j - 1], swap(across[j - 1], 1)])
        part = partial_input_grad(turn, pieces[j], mean_weight, perturbed, slab_sign[j], 4, VMEM_LIMIT_GRAD)
        passed = cross(part[2], 1)
        if j == 1:
            passed, owned[2], blocks[1] = tie(passed, owned[2], blocks[1])
            total = sum(x.astype(jnp.float32) for x in owned)
        parts = scatter(part, passed)
        parts[0], hopped = tie(parts[0], hopped)
        slab_inputs.append(hopped)
        if j == n_depth - 1:
            grads = weight_grads(turn, pieces, slab_inputs, slab_sign, noise, scale, 0, [])
            parts, grads = tie(parts, grads)
        part = sum(x.astype(jnp.float32) for x in parts).astype(jnp.bfloat16)
        total += hop(part, n_depth - j).astype(jnp.float32)
    input_grad = total.astype(jnp.bfloat16)
    grads = weight_grads(turn, pieces, slab_inputs, slab_sign, noise, scale, 1, grads)
    mean_grad, sigma_grad = grads
    return (input_grad, mean_grad, sigma_grad)


def solution(mesh):
    return jax.shard_map(
        local,
        mesh=mesh,
        in_specs=(
            P(("depth", "col"), "row"),
            P(("depth", "col"), "row"),
            P(("depth", "row"), "col"),
            P(("depth", "row"), "col"),
            P(("col", "depth"), "row"),
            P(("col", "depth"), "row"),
            P(("col", "depth"), "row"),
        ),
        out_specs=(
            P(("depth", "col"), "row"),
            P(("col", "depth"), "row"),
            P(("col", "depth"), "row"),
        ),
        check_vma=False,
    )
```

```python
import functools

import jax
import jax.numpy as jnp
from jax import lax
from jax.experimental import pallas as pl
from jax.experimental.pallas import tpu as pltpu
from jax.sharding import PartitionSpec as P

VMEM_LIMIT = 22 * 1024 * 1024
VMEM_LIMIT_GRAD = 14 * 1024 * 1024
OWN_LIMIT = 50 * 1024 * 1024
ORDER = (0, 1, 3, 2)


def grad_kernel(n_piece, turn_ref, *refs):
    pieces, (mean_ref, pert_ref, head_ref, tail_ref) = refs[:n_piece], refs[n_piece:n_piece + 4]
    outs, (both, sems) = refs[n_piece + 4:-2], refs[-2:]

    @pl.when(pl.program_id(0) == 0)
    def _():
        copies = [
            pltpu.make_async_copy(pieces[k], both.at[turn_ref[0] ^ k], sems.at[k])
            for k in range(n_piece)
        ]
        for copy in copies:
            copy.start()
        for copy in copies:
            copy.wait()

    rows, hidden = both.shape[2:]
    grads = both[:, 0].reshape(n_piece * rows, hidden)
    signed = both[:, 1].reshape(n_piece * rows, hidden)
    part_a = jnp.dot(grads, mean_ref[...], preferred_element_type=jnp.float32)
    part_b = jnp.dot(signed, pert_ref[...], preferred_element_type=jnp.float32)
    for k in range(n_piece):
        at = slice(k * rows, (k + 1) * rows)
        block = ORDER.index(k)
        sign = (head_ref[block] if block < n_piece - 1 else tail_ref[...]).astype(jnp.float32)
        outs[k][...] = (part_a[at] + part_b[at] * sign).astype(outs[k].dtype)


def partial_input_grad(turn, pieces, mean_weight, perturbed, signs, weight, limit):
    hidden, feats = mean_weight.shape
    n_piece, rows = len(pieces), pieces[0].shape[1]
    tile = min(256, feats)
    any_spec = pl.BlockSpec(memory_space=pl.ANY)
    weight_spec = pl.BlockSpec((hidden, tile), lambda f, turn: (0, f))
    block_spec = pl.BlockSpec((rows, tile), lambda f, turn: (0, f))
    return pl.pallas_call(
        functools.partial(grad_kernel, n_piece),
        grid_spec=pltpu.PrefetchScalarGridSpec(
            num_scalar_prefetch=1,
            grid=(feats // tile,),
            in_specs=[any_spec] * n_piece
            + [weight_spec, weight_spec, pl.BlockSpec((n_piece - 1, rows, tile), lambda f, turn: (0, 0, f)), block_spec],
            out_specs=[block_spec] * n_piece,
            scratch_shapes=[
                pltpu.VMEM((n_piece,) + pieces[0].shape, jnp.bfloat16),
                pltpu.SemaphoreType.DMA((n_piece,)),
            ],
        ),
        out_shape=[jax.ShapeDtypeStruct((rows, feats), jnp.bfloat16)] * n_piece,
        compiler_params=pltpu.CompilerParams(vmem_limit_bytes=limit),
        cost_estimate=pl.CostEstimate(
            flops=int(weight * n_piece * rows * hidden * feats),
            bytes_accessed=4 * (n_piece * rows * (hidden + feats) + hidden * feats),
            transcendentals=0,
        ),
        name="input_grad",
    )(turn, *pieces, mean_weight, perturbed, *signs)


def weight_kernel(n_slab, n_piece, scale, turn_ref, *refs):
    n_grads = n_slab * n_piece
    grads, inputs, signs = refs[:n_grads], refs[n_grads:n_grads + 2 * n_slab], refs[n_grads + 2 * n_slab:n_grads + 4 * n_slab]
    noise_ref, (mean_ref, sigma_ref, plain, signed) = refs[n_grads + 4 * n_slab], refs[-4:]
    rows = grads[0].shape[1]

    @pl.when(pl.program_id(1) == 0)
    def _():
        for j in range(n_slab):
            for i, k in enumerate(ORDER):
                to = pl.ds(pl.multiple_of((j * n_piece + (k ^ turn_ref[0])) * rows, rows), rows)
                value, sign = (
                    group[2 * j][i] if i < n_piece - 1 else group[2 * j + 1][...] for group in (inputs, signs)
                )
                plain[to, :] = value
                signed[to, :] = value * sign

    dims = (((0,), (0,)), ((), ()))
    grad = jnp.concatenate([g[0] for g in grads], axis=0)
    mean = lax.dot_general(grad, plain[...], dims, preferred_element_type=jnp.float32)
    mean_ref[...] = mean * scale
    grad = jnp.concatenate([g[1] for g in grads], axis=0)
    sigma = lax.dot_general(grad, signed[...], dims, preferred_element_type=jnp.float32)
    sigma_ref[...] = sigma * scale * noise_ref[...].astype(jnp.float32)


def weight_grads(turn, pieces, inputs, signs, noise, scale, part, partial):
    n_slab, n_piece = len(pieces), len(pieces[0])
    hidden, feats = noise.shape
    rows = pieces[0][0].shape[1]
    tokens = n_slab * n_piece * rows
    width = feats if tokens <= 1280 else min(256, feats)
    tile = 256 if hidden % 256 == 0 else hidden
    cut = (hidden // tile + 1) // 2
    first, steps = (0, cut) if part == 0 else (cut, hidden // tile - cut)
    if not steps:
        return partial
    grad_spec = pl.BlockSpec((2, rows, tile), lambda f, h, turn: (0, 0, h + first))
    out_spec = pl.BlockSpec((tile, width), lambda f, h, turn: (h + first, f))
    inputs, signs = ([x for slab in group for x in slab] for group in (inputs, signs))
    operands = [p for slab_pieces in pieces for p in slab_pieces] + inputs + signs + [noise]
    return pl.pallas_call(
        functools.partial(weight_kernel, n_slab, n_piece, scale),
        grid_spec=pltpu.PrefetchScalarGridSpec(
            num_scalar_prefetch=1,
            grid=(feats // width, steps),
            in_specs=[grad_spec] * (n_slab * n_piece)
            + [
                pl.BlockSpec(x.shape[:-1] + (width,), lambda f, h, turn, lead=x.ndim - 1: (0,) * lead + (f,))
                for x in inputs + signs
            ]
            + [out_spec]
            + [pl.BlockSpec(memory_space=pl.ANY)] * len(partial),
            out_specs=[out_spec, out_spec],
            scratch_shapes=[
                pltpu.VMEM((tokens, width), jnp.bfloat16),
                pltpu.VMEM((tokens, width), jnp.bfloat16),
            ],
        ),
        out_shape=[jax.ShapeDtypeStruct((hidden, feats), jnp.float32)] * 2,
        input_output_aliases={1 + len(operands) + i: i for i in range(len(partial))},
        compiler_params=pltpu.CompilerParams(vmem_limit_bytes=VMEM_LIMIT),
        cost_estimate=pl.CostEstimate(
            flops=4 * tokens * tile * steps * feats if part else 1,
            bytes_accessed=4 * (tokens * tile * steps + tokens * feats) + 10 * tile * steps * feats if part else 1,
            transcendentals=0,
        ),
        name="weight_grads",
    )(turn, *operands, *partial)


def local(inputs, in_bits, out_grads, out_bits, mean_weight, sigma_weight, noise):
    n_depth, n_row, n_col = (lax.axis_size(a) for a in ("depth", "row", "col"))
    depth, row, col = (lax.axis_index(a) for a in ("depth", "row", "col"))
    hidden = mean_weight.shape[0]
    scale = (inputs.shape[0] * n_col * n_depth) ** (-0.5)
    turn = (row ^ col).astype(jnp.int32).reshape(1)

    def hop(value, step):
        return lax.ppermute(value, "depth", [(i, (i + step) % n_depth) for i in range(n_depth)])

    def swap(value, bit):
        return lax.ppermute(value, "row", [(i, i ^ bit) for i in range(n_row)])

    def cross(value, bits):
        return lax.ppermute(value, "col", [(i, i ^ bits) for i in range(n_col)])

    def half(step):
        start = ((depth + step) % n_depth) * hidden
        grads, bits = (lax.dynamic_slice_in_dim(a, start, hidden, 1) for a in (out_grads, out_bits))
        return jnp.stack([grads, grads * (1 - 2 * bits).astype(jnp.bfloat16)])

    def tie(*values):
        return lax.optimization_barrier(values)

    mine, others = half(0), [half(j) for j in range(1, n_depth)]
    others, in_bits = tie(others, in_bits)
    in_sign = (1 - 2 * in_bits).astype(jnp.bfloat16)
    perturbed = (sigma_weight.astype(jnp.float32) * noise.astype(jnp.float32)).astype(jnp.bfloat16)

    others = [hop(other, j + 1) for j, other in enumerate(others)]
    signs = [in_sign, cross(in_sign, 1), None, cross(in_sign, 3)]
    signs[1], signs[3] = tie(signs[1], signs[3])
    signs[2] = cross(signs[3], 1)
    across, others, perturbed, signs, inputs = tie(swap(mine, 2), others, perturbed, signs, inputs)
    head, tail = jnp.stack([signs[0], signs[1], signs[3]]), signs[2]
    head, late_inputs = tie(head, inputs)
    pieces = [[mine, swap(mine, 1), across, swap(across, 1)]]

    slab_sign = [[head, tail]] + [[hop(head, j), hop(tail, j)] for j in range(1, n_depth)]
    own = partial_input_grad(turn, pieces[0], mean_weight, perturbed, slab_sign[0], 64, OWN_LIMIT)
    blocks = [inputs, cross(inputs, 1), None, cross(late_inputs, 3)]
    blocks[1], own = tie(blocks[1], own)
    passed = cross(own[2], 1)
    across = [swap(other, 2) for other in others]
    across, slab_sign, blocks[1], blocks[3], passed = tie(across, slab_sign, blocks[1], blocks[3], passed)
    three, blocks[3] = tie(jnp.stack([blocks[0], blocks[1], blocks[3]]), blocks[3])
    blocks = [three, cross(blocks[3], 1)]

    def scatter(part, passed):
        joined = (part[3].astype(jnp.float32) + passed.astype(jnp.float32)).astype(jnp.bfloat16)
        return [part[0], cross(part[1], 1), cross(joined, 3)]

    owned = scatter(own, passed)
    slab_inputs = [blocks]
    total, grads = None, []
    for j in range(1, n_depth):
        hopped = [hop(x, j) for x in blocks]
        pieces.append([others[j - 1], swap(others[j - 1], 1), across[j - 1], swap(across[j - 1], 1)])
        part = partial_input_grad(turn, pieces[j], mean_weight, perturbed, slab_sign[j], 4, VMEM_LIMIT_GRAD)
        passed = cross(part[2], 1)
        if j == 1:
            passed, owned[2], blocks[1] = tie(passed, owned[2], blocks[1])
            total = sum(x.astype(jnp.float32) for x in owned)
        parts = scatter(part, passed)
        parts[0], hopped = tie(parts[0], hopped)
        slab_inputs.append(hopped)
        if j == n_depth - 1:
            grads = weight_grads(turn, pieces, slab_inputs, slab_sign, noise, scale, 0, [])
            parts, grads = tie(parts, grads)
        part = sum(x.astype(jnp.float32) for x in parts).astype(jnp.bfloat16)
        total += hop(part, n_depth - j).astype(jnp.float32)
    input_grad = total.astype(jnp.bfloat16)
    grads = weight_grads(turn, pieces, slab_inputs, slab_sign, noise, scale, 1, grads)
    mean_grad, sigma_grad = grads
    return (input_grad, mean_grad, sigma_grad)


def solution(mesh):
    return jax.shard_map(
        local,
        mesh=mesh,
        in_specs=(
            P(("depth", "col"), "row"),
            P(("depth", "col"), "row"),
            P(("depth", "row"), "col"),
            P(("depth", "row"), "col"),
            P(("col", "depth"), "row"),
            P(("col", "depth"), "row"),
            P(("col", "depth"), "row"),
        ),
        out_specs=(
            P(("depth", "col"), "row"),
            P(("col", "depth"), "row"),
            P(("col", "depth"), "row"),
        ),
        check_vma=False,
    )
```
